32 devices in a mesh: win: 4 (over x, core), srow: 4 (over z), scol: 2 (over y).
Axes of the slice: x: 2, y: 2, z: 4, core: 2. Of those that a mesh axis runs over, the one named last changes fastest.
Arguments:
- spectra: float32 [4, 2, 64, 4096], P(None, None, 'win', ('srow', 'scol')), may hold values from -6 to 6
- bins: int32 [4], replicated, may hold values from 1 to 2047
- travel: int32 [4096, 2048], P(('srow', 'scol'), 'win'), may hold values from 0 to 16383
Outputs:
- coherence: bfloat16 [4, 2, 4096, 4, 1024], P('win', None, 'srow', None, 'scol')
- beam: float32 [4, 2048], P('win')
The draws below stay inside these ranges and needn't reach their ends.
All inputs are finite; a program needn't handle non-finite values.
Results may differ from the reference program's by a relative error of at most 0.012.
Values may be sent and summed in bfloat16 or wider, within the bound.
A program may use at most 128 MiB of HBM per device.

```python
import math
import jax
import jax.numpy as jnp
from jax import lax

S = 4096
F = 4
P_SIZE = 2048
NFFT = 4096
TMAX = 16384
W = 64
BLOCK = 1024


def plant(result, stream_key, low, top_value):
    longest = result.shape.index(max(result.shape))
    spots = []
    for shift in (0, 1):
        where = [jax.random.randint(jax.random.fold_in(stream_key, axis), (), 0, length) for axis, length in enumerate(result.shape)]
        where[longest] = (where[longest] + shift) % result.shape[longest]
        spots.append(tuple(where))
    return result.at[spots[0]].set(low).at[spots[1]].set(top_value)


def steps_of(rng, dims, cuts, low, high):
    factor_of = 1.0
    for dim, parts in cuts:
        steps = jax.random.uniform(jax.random.fold_in(jax.random.fold_in(rng, 6), dim), (parts,), jnp.float32, low / len(cuts), high / len(cuts))
        factor_of = factor_of * jnp.repeat(jnp.exp(steps), dims[dim] // parts).reshape((-1,) + (1,) * (len(dims) - 1 - dim))
    return factor_of


def gaussian(rng, shape, scale, bound, pieces=(), dtype=jnp.bfloat16):
    level = steps_of(rng, shape, pieces, -0.22, 0.18) if pieces else 1.0
    entries = jax.random.normal(rng, shape, jnp.float32) * scale * level
    return jnp.minimum(jnp.maximum(entries, -bound), bound).astype(dtype)


def setup_inputs(seed: int = 0) -> dict:
    key_list = jax.random.split(jax.random.key(seed), 4)
    spectra = gaussian(key_list[0], (F, 2, W, S), 1.0, 6.0, ((2, 4), (3, 8)), jnp.float32)
    bins = plant(jax.random.randint(key_list[1], (F,), 1, NFFT // 2), jax.random.fold_in(key_list[1], 1), 1, (NFFT // 2) - 1).astype(jnp.int32)
    travel = plant(jax.random.randint(key_list[2], (S, P_SIZE), 0, TMAX), jax.random.fold_in(key_list[2], 1), 0, TMAX - 1).astype(jnp.int32)
    return dict(spectra=spectra, bins=bins, travel=travel)


def reference(spectra, bins, travel):
    magnitude = jnp.sqrt(spectra[:, 0] * spectra[:, 0] + spectra[:, 1] * spectra[:, 1] + 0.5)
    normal = (spectra / magnitude[:, None]).astype(jnp.bfloat16).astype(jnp.float32)
    highest = lax.Precision.HIGHEST

    def one_freq(inputs):
        piece, bin_index = inputs
        real = jnp.dot(piece[0].T, piece[0], precision=highest) + jnp.dot(piece[1].T, piece[1], precision=highest)
        imag = jnp.dot(piece[1].T, piece[0], precision=highest) - jnp.dot(piece[0].T, piece[1], precision=highest)
        extent = jnp.sqrt(real * real + imag * imag + float(W))
        coh_real = (real / extent).astype(jnp.bfloat16)
        coh_imag = (imag / extent).astype(jnp.bfloat16)
        cycles = bin_index * travel % NFFT
        angle = 2.0 * math.pi / NFFT * cycles.astype(jnp.float32)
        steer_real = jnp.cos(angle).astype(jnp.bfloat16).astype(jnp.float32)
        steer_imag = (-jnp.sin(angle)).astype(jnp.bfloat16).astype(jnp.float32)
        kreal = coh_real.astype(jnp.float32)
        kimag = coh_imag.astype(jnp.float32)
        image_real = jnp.dot(kreal, steer_real, precision=highest) - jnp.dot(kimag, steer_imag, precision=highest)
        image_imag = jnp.dot(kreal, steer_imag, precision=highest) + jnp.dot(kimag, steer_real, precision=highest)
        power = lax.optimization_barrier(jnp.sum(steer_real * image_real + steer_imag * image_imag, axis=0)) / S
        stacked = jnp.stack([coh_real, coh_imag]).reshape(2, S, S // BLOCK, BLOCK)
        return (stacked, power)
    coherence, beam = lax.map(one_freq, (normal, bins))
    return (coherence, beam)
```

```python
import functools
import math

import jax
import jax.numpy as jnp
import numpy as np
from jax import lax
from jax.experimental import pallas as pl
from jax.experimental.pallas import tpu as pltpu
from jax.sharding import PartitionSpec as P

NFFT = 4096
MESH = pl.DeviceIdType.MESH
MAGIC = 12582912.0
ROWS = 256


def phase_normalized(spectra):
    magnitude = jnp.sqrt(spectra[:, 0] * spectra[:, 0] + spectra[:, 1] * spectra[:, 1] + 0.5)
    return (spectra / magnitude[:, None]).astype(jnp.bfloat16)


def fitted():
    nodes = 0.25 * (1.0 - np.cos(np.pi * (np.arange(64) + 0.5) / 64)) / 2.0
    root = np.sqrt(nodes)
    powers = np.vander(nodes, 5, increasing=True)
    sine = np.linalg.lstsq(powers, np.sin(np.pi * root) / root, rcond=None)[0]
    cosine = np.linalg.lstsq(powers, -2.0 * np.cos(np.pi * root), rcond=None)[0]
    return [float(a) for a in sine], [float(a) for a in cosine]


def steer(travel, scale):
    sine, cosine = fitted()
    turns = travel.astype(jnp.int32).astype(jnp.float32) * scale
    rest = turns - ((turns + MAGIC) - MAGIC)
    z = rest * rest
    s = sine[4]
    c = cosine[4]
    for k in (3, 2, 1, 0):
        s = s * z + sine[k]
        c = c * z + cosine[k]
    s = s * rest
    return 1.0 - 2.0 * (s * s), s * c


def exchange_kernel(nw, nr, nc, x_ref, t_ref, xloc, xg, tcol, trow, send, recv, local):
    w, r, c = lax.axis_index("win"), lax.axis_index("srow"), lax.axis_index("scol")
    core = lax.rem(w, 2)
    mate = {"win": w + 1 - 2 * core}
    number = {}

    def slot(*name):
        return number.setdefault(name, len(number))

    def make(name, src, dst, where):
        k = slot(*name)
        return pltpu.make_async_remote_copy(
            src_ref=src, dst_ref=dst, send_sem=send.at[k], recv_sem=recv.at[k],
            device_id=where, device_id_type=MESH,
        )

    pending = []

    def start(cond, name, src, dst, where):
        copy = make(name, src, dst, where)
        if cond is True:
            copy.start()
        else:
            pl.when(cond)(copy.start)
        pending.append((cond, copy))

    def arrived(cond, name, dst):
        copy = make(name, dst, dst, mate)
        if cond is True:
            copy.wait_recv()
        else:
            pl.when(cond)(copy.wait_recv)

    barrier = pltpu.get_barrier_semaphore()

    def greet(where):
        pl.semaphore_signal(barrier, inc=1, device_id=where, device_id_type=MESH)

    pl.when(r > 0)(lambda: greet({"srow": r - 1}))
    pl.when(r < nr - 1)(lambda: greet({"srow": r + 1}))
    for d in range(1, nc):
        greet({"scol": lax.rem(c + d, nc)})
    for d in range(1, nw):
        greet({"win": lax.rem(w + d, nw)})
    ends = jnp.where(r > 0, 1, 0) + jnp.where(r < nr - 1, 1, 0)
    pl.semaphore_wait(barrier, ends + nc - 1 + nw - 1)

    locals_x = [
        pltpu.make_async_copy(x_ref, xloc.at[r], local.at[0]),
        pltpu.make_async_copy(x_ref, xloc.at[nr + c], local.at[1]),
    ]
    locals_t = [
        pltpu.make_async_copy(t_ref.at[0], tcol.at[core, 0, 0], local.at[2]),
        pltpu.make_async_copy(t_ref.at[1], tcol.at[core, 1, 0], local.at[3]),
        pltpu.make_async_copy(t_ref, trow.at[core, c], local.at[4]),
    ]

    def chain_x(s):
        start((r < nr - 1) & (r >= s), ("xu", s + 1),
              x_ref if s == 0 else xloc.at[jnp.maximum(r - s, 0)],
              xloc.at[jnp.maximum(r - s, 0)], {"srow": r + 1})
        start((r > 0) & (r + s < nr), ("xd", s + 1),
              x_ref if s == 0 else xloc.at[jnp.minimum(r + s, nr - 1)],
              xloc.at[jnp.minimum(r + s, nr - 1)], {"srow": r - 1})

    def chain_t(s):
        start((r < nr - 1) & (r >= s), ("tu", s + 1),
              t_ref.at[0] if s == 0 else tcol.at[core, 0, s],
              tcol.at[core, 0, s + 1], {"srow": r + 1})
        start((r > 0) & (r + s < nr), ("td", s + 1),
              t_ref.at[1] if s == 0 else tcol.at[core, 1, s],
              tcol.at[core, 1, s + 1], {"srow": r - 1})

    chain_x(0)
    for d in range(1, nc):
        start(True, ("xc", d), x_ref, xloc.at[nr + c], {"scol": lax.rem(c + d, nc)})
    chain_t(0)
    for d in range(1, nc):
        start(True, ("tc", d), t_ref, trow.at[core, c], {"scol": lax.rem(c + d, nc)})
    for copy in locals_x + locals_t:
        copy.start()
    for h in range(2):
        start(True, ("p", h, 0), t_ref.at[h], tcol.at[core, h, 0], mate)
    for s in range(1, nr):
        arrived(r >= s, ("xu", s), xloc.at[jnp.maximum(r - s, 0)])
        arrived(r + s < nr, ("xd", s), xloc.at[jnp.minimum(r + s, nr - 1)])
        if s < nr - 1:
            chain_x(s)
    for d in range(1, nc):
        arrived(True, ("xc", d), xloc.at[nr + lax.rem(c + nc - d, nc)])
    for copy in locals_x:
        copy.wait()
    for d in range(1, nw):
        to = lax.rem(w + d, nw)
        start(True, ("xw", d), xloc.at[:, lax.rem(to, 2)], xg.at[w], {"win": to})
    own = pltpu.make_async_copy(xloc.at[:, core], xg.at[w], local.at[5])
    own.start()
    for d in range(1, nc):
        arrived(True, ("tc", d), trow.at[core, lax.rem(c + nc - d, nc)])
    for copy in locals_t:
        copy.wait()
    start(True, ("pr",), trow.at[core], trow.at[core], mate)
    for s in range(1, nr):
        arrived(r >= s, ("tu", s), tcol.at[core, 0, s])
        arrived(r + s < nr, ("td", s), tcol.at[core, 1, s])
        if s < nr - 1:
            chain_t(s)
        start(r >= s, ("p", 0, s), tcol.at[core, 0, s], tcol.at[core, 0, s], mate)
        start(r + s < nr, ("p", 1, s), tcol.at[core, 1, s], tcol.at[core, 1, s], mate)
    for d in range(1, nw):
        arrived(True, ("xw", d), xg.at[lax.rem(w + nw - d, nw)])
    own.wait()
    arrived(True, ("pr",), trow.at[1 - core])
    for s in range(nr):
        arrived(True if s == 0 else r >= s, ("p", 0, s), tcol.at[1 - core, 0, s])
        arrived(True if s == 0 else r + s < nr, ("p", 1, s), tcol.at[1 - core, 1, s])
    for cond, copy in pending:
        if cond is True:
            copy.wait_send()
        else:
            pl.when(cond)(copy.wait_send)


def exchange(x, t, nw, nr, nc):
    half_f, wl, n = x.shape[1], x.shape[3], x.shape[4]
    ph = t.shape[2]
    count = 4 * nr + 2 * nc + nw + 2 * nr + 2
    anywhere = pl.BlockSpec(memory_space=pl.ANY)
    return pl.pallas_call(
        functools.partial(exchange_kernel, nw, nr, nc),
        out_shape=(
            jax.ShapeDtypeStruct((nr + nc, 2, half_f, 2, wl, n), x.dtype),
            jax.ShapeDtypeStruct((nw, nr + nc, half_f, 2, wl, n), x.dtype),
            jax.ShapeDtypeStruct((2, 2, nr, n, ph), t.dtype),
            jax.ShapeDtypeStruct((2, nc, 2, n, ph), t.dtype),
        ),
        in_specs=[anywhere] * 2,
        out_specs=(anywhere,) * 4,
        scratch_shapes=[
            pltpu.SemaphoreType.DMA((count,)),
            pltpu.SemaphoreType.DMA((count,)),
            pltpu.SemaphoreType.DMA((6,)),
        ],
        compiler_params=pltpu.CompilerParams(collective_id=0, has_side_effects=True),
        name="exchange",
    )(x, t)


def beam_kernel(nr, nc, total, info, xrow, xcr, xci, tcol, trow, coh, part, kscr, csteer, rsteer):
    fi, t = pl.program_id(0), pl.program_id(1)
    r = info[0]
    scale = info[2 + fi].astype(jnp.float32) * (1.0 / NFFT)
    rows = xrow.shape[1]
    n, ph = tcol.shape[3], tcol.shape[4]
    step = 32

    @pl.when((fi == 0) & (t == 0))
    def _():
        part[...] = jnp.zeros_like(part)

    for slab in range(2):
        @pl.loop(0, n // step)
        def _(i):
            at = pl.ds(pl.multiple_of(i * step, step), step)
            cr, ci = steer(tcol[slab, 0, 0, at, :], scale)
            cr, ci = cr.astype(jnp.bfloat16), ci.astype(jnp.bfloat16)
            csteer[0, slab, at, :] = cr
            csteer[1, slab, at, :] = ci
            csteer[2, slab, at, :] = cr + ci

    @pl.when((t == 0) | (t == r + 1))
    def _():
        for slab in range(2):
            for block in range(nc):
                @pl.loop(0, n // step)
                def _(i):
                    at = pl.ds(pl.multiple_of(i * step, step), step)
                    to = pl.ds(pl.multiple_of(block * n + i * step, step), step)
                    rr, ri = steer(trow[slab, block, 0, at, :], scale)
                    rsteer[0, slab, to, :] = rr.astype(jnp.bfloat16).astype(jnp.float32)
                    rsteer[1, slab, to, :] = ri.astype(jnp.bfloat16).astype(jnp.float32)

    chunk = min(ROWS, rows)

    @pl.when(t != r + 1)
    def _():
        @pl.loop(0, rows // chunk)
        def _(m):
            at = pl.ds(pl.multiple_of(m * chunk, chunk), chunk)
            left = xrow[0, at, :]
            re = jnp.dot(left, xcr[0, 0], preferred_element_type=jnp.float32)
            im = jnp.dot(left, xci[0, 0], preferred_element_type=jnp.float32)
            inverse = lax.rsqrt(re * re + im * im + float(total))
            kr = (re * inverse).astype(jnp.bfloat16)
            ki = (im * inverse).astype(jnp.bfloat16)
            kscr[0, at, :] = kr
            kscr[1, at, :] = ki
            kscr[2, at, :] = kr + ki

            @pl.when(fi == 0)
            def _():
                coh[0, at, :] = kr
                coh[1, at, :] = ki

    half = jnp.where(t <= r, 0, 1)
    weight = jnp.where((t == r) | (t == r + 1), 1.0, 2.0)

    @pl.loop(0, rows // chunk)
    def _(m):
        at = pl.ds(pl.multiple_of(m * chunk, chunk), chunk)
        for slab in range(2):
            t1 = jnp.dot(kscr[0, at, :], csteer[0, slab], preferred_element_type=jnp.float32)
            t2 = jnp.dot(kscr[1, at, :], csteer[1, slab], preferred_element_type=jnp.float32)
            t3 = jnp.dot(kscr[2, at, :], csteer[2, slab], preferred_element_type=jnp.float32)
            v = rsteer[0, slab, at, :] * (t1 - t2) + rsteer[1, slab, at, :] * (t3 - (t1 + t2))
            v = jnp.sum(v.reshape(chunk // 8, 8, ph), axis=0)
            part[fi, half, slab] += weight * v


def beam_call(info, xrow, xcr, xci, tcol, trow, total):
    half_f, rows, depth = xrow.shape
    nr, n = xcr.shape[1], xcr.shape[3]
    nc, ph = trow.shape[1], trow.shape[4]

    def freq(fi, info):
        return lax.rem(info[1] + fi, half_f)

    def plane(t, info):
        return jnp.where(t <= info[0], t, t - 1)

    def col_map(fi, t, info):
        return (freq(fi, info), plane(t, info), 0, 0)

    def tcol_map(fi, t, info):
        r = info[0]
        return (0, jnp.where(t <= r, 0, 1), jnp.where(t <= r, r - t, t - 1 - r), 0, 0)

    def coh_map(fi, t, info):
        return (0, 0, jnp.where(fi == 0, plane(t, info), nr - 1))

    return pl.pallas_call(
        functools.partial(beam_kernel, nr, nc, total),
        out_shape=(
            jax.ShapeDtypeStruct((2, rows, nr * n), jnp.bfloat16),
            jax.ShapeDtypeStruct((half_f, 2, 2, 8, ph), jnp.float32),
        ),
        grid_spec=pltpu.PrefetchScalarGridSpec(
            num_scalar_prefetch=1,
            grid=(half_f, nr + 1),
            in_specs=[
                pl.BlockSpec((1, rows, depth), lambda fi, t, info: (freq(fi, info), 0, 0)),
                pl.BlockSpec((1, 1, depth, n), col_map),
                pl.BlockSpec((1, 1, depth, n), col_map),
                pl.BlockSpec((2, 1, 1, n, ph), tcol_map),
                pl.BlockSpec(
                    (2, nc, 1, n, ph),
                    lambda fi, t, info: (0, 0, jnp.where(t <= info[0], 0, 1), 0, 0),
                ),
            ],
            out_specs=(
                pl.BlockSpec((2, rows, n), coh_map),
                pl.BlockSpec((half_f, 2, 2, 8, ph), lambda fi, t, info: (0, 0, 0, 0, 0)),
            ),
            scratch_shapes=[
                pltpu.VMEM((3, rows, n), jnp.bfloat16),
                pltpu.VMEM((3, 2, n, ph), jnp.bfloat16),
                pltpu.VMEM((2, 2, rows, ph), jnp.float32),
            ],
        ),
        compiler_params=pltpu.CompilerParams(
            dimension_semantics=("arbitrary", "arbitrary"), vmem_limit_bytes=50 * 2**20
        ),
        name="beam",
    )(info, xrow, xcr, xci, tcol, trow)


def body(nw, nr, nc, spectra, bins, travel):
    w, r, c = lax.axis_index("win"), lax.axis_index("srow"), lax.axis_index("scol")
    group, core = w // 2, w % 2
    nf, _, wl, n = spectra.shape
    half_f = nf // 2
    ph = travel.shape[1] // 2
    x = phase_normalized(spectra).reshape(half_f, 2, 2, wl, n).swapaxes(0, 1)
    t = (travel % NFFT).astype(jnp.int16).reshape(n, 2, ph).swapaxes(0, 1)
    _, xg, tcol, trow = exchange(x, t, nw, nr, nc)
    cols = xg[:, :nr].transpose(2, 1, 3, 0, 4, 5)
    xcr = cols.reshape(half_f, nr, 2 * nw * wl, n)
    xci = jnp.stack([-cols[:, :, 1], cols[:, :, 0]], axis=2).reshape(half_f, nr, 2 * nw * wl, n)
    xrow = xg[:, nr:].transpose(2, 1, 5, 3, 0, 4).reshape(half_f, nc * n, 2 * nw * wl)
    info = jnp.concatenate([
        jnp.stack([r, group]).astype(jnp.int32),
        jnp.stack([bins[(group + i) % half_f * 2 + core] for i in range(half_f)]),
    ])
    coherent, part = beam_call(info, xrow, xcr, xci, tcol, trow, nw * wl)
    part = part.sum(axis=3).swapaxes(1, 2).reshape(half_f, 2 * 2 * ph)
    spread = jnp.zeros((nf, (nw // 2) * 4 * ph), jnp.float32)
    for i in range(half_f):
        spread = lax.dynamic_update_slice(
            spread, part[i : i + 1], ((group + i) % half_f * 2 + core, group * 4 * ph)
        )
    power = lax.psum(spread, ("win", "srow", "scol")) / (nr * nc * n)
    beam = lax.dynamic_slice_in_dim(power, w, 1, axis=0)
    return coherent.reshape(1, 2, nc * n, nr, n), beam


def solution(mesh):
    sizes = [mesh.shape[a] for a in ("win", "srow", "scol")]
    placed = (P(None, None, "win", ("srow", "scol")), P(), P(("srow", "scol"), "win"))
    return jax.shard_map(
        functools.partial(body, *sizes),
        mesh=mesh,
        in_specs=placed,
        out_specs=(P("win", None, "srow", None, "scol"), P("win", None)),
        check_vma=False,
    )
```

```python
import functools
import math

import jax
import jax.numpy as jnp
import numpy as np
from jax import lax
from jax.experimental import pallas as pl
from jax.experimental.pallas import tpu as pltpu
from jax.sharding import PartitionSpec as P

NFFT = 4096
MESH = pl.DeviceIdType.MESH
MAGIC = 12582912.0
ROWS = 256


def phase_normalized(spectra):
    magnitude = jnp.sqrt(spectra[:, 0] * spectra[:, 0] + spectra[:, 1] * spectra[:, 1] + 0.5)
    return (spectra / magnitude[:, None]).astype(jnp.bfloat16)


def fitted():
    nodes = 0.25 * (1.0 - np.cos(np.pi * (np.arange(64) + 0.5) / 64)) / 2.0
    root = np.sqrt(nodes)
    powers = np.vander(nodes, 5, increasing=True)
    sine = np.linalg.lstsq(powers, np.sin(np.pi * root) / root, rcond=None)[0]
    cosine = np.linalg.lstsq(powers, -2.0 * np.cos(np.pi * root), rcond=None)[0]
    return [float(a) for a in sine], [float(a) for a in cosine]


def steer(travel, scale):
    sine, cosine = fitted()
    turns = travel.astype(jnp.int32).astype(jnp.float32) * scale
    rest = turns - ((turns + MAGIC) - MAGIC)
    z = rest * rest
    s = sine[4]
    c = cosine[4]
    for k in (3, 2, 1, 0):
        s = s * z + sine[k]
        c = c * z + cosine[k]
    s = s * rest
    return 1.0 - 2.0 * (s * s), s * c


def exchange_kernel(nw, nr, nc, x_ref, t_ref, xg, tcol, trow, xloc, send, recv, local):
    w, r, c = lax.axis_index("win"), lax.axis_index("srow"), lax.axis_index("scol")
    core = lax.rem(w, 2)
    mate = {"win": w + 1 - 2 * core}
    number = {}

    def slot(*name):
        return number.setdefault(name, len(number))

    def make(name, src, dst, where):
        k = slot(*name)
        return pltpu.make_async_remote_copy(
            src_ref=src, dst_ref=dst, send_sem=send.at[k], recv_sem=recv.at[k],
            device_id=where, device_id_type=MESH,
        )

    pending = []

    def start(cond, name, src, dst, where):
        copy = make(name, src, dst, where)
        if cond is True:
            copy.start()
        else:
            pl.when(cond)(copy.start)
        pending.append((cond, copy))

    def arrived(cond, name, dst):
        copy = make(name, dst, dst, mate)
        if cond is True:
            copy.wait_recv()
        else:
            pl.when(cond)(copy.wait_recv)

    barrier = pltpu.get_barrier_semaphore()

    def greet(where):
        pl.semaphore_signal(barrier, inc=1, device_id=where, device_id_type=MESH)

    pl.when(r > 0)(lambda: greet({"srow": r - 1}))
    pl.when(r < nr - 1)(lambda: greet({"srow": r + 1}))
    for d in range(1, nc):
        greet({"scol": lax.rem(c + d, nc)})
    for d in range(1, nw):
        greet({"win": lax.rem(w + d, nw)})
    ends = jnp.where(r > 0, 1, 0) + jnp.where(r < nr - 1, 1, 0)
    pl.semaphore_wait(barrier, ends + nc - 1 + nw - 1)

    locals_t = [
        pltpu.make_async_copy(t_ref.at[0], tcol.at[core, 0, 0], local.at[0]),
        pltpu.make_async_copy(t_ref.at[1], tcol.at[core, 1, 0], local.at[1]),
        pltpu.make_async_copy(t_ref, trow.at[core, c], local.at[2]),
    ]

    def chain_x(s):
        start((r < nr - 1) & (r >= s), ("xu", s + 1),
              x_ref if s == 0 else xloc.at[jnp.maximum(r - s, 0)],
              xloc.at[jnp.maximum(r - s, 0)], {"srow": r + 1})
        start((r > 0) & (r + s < nr), ("xd", s + 1),
              x_ref if s == 0 else xloc.at[jnp.minimum(r + s, nr - 1)],
              xloc.at[jnp.minimum(r + s, nr - 1)], {"srow": r - 1})

    def chain_t(s):
        start((r < nr - 1) & (r >= s), ("tu", s + 1),
              t_ref.at[0] if s == 0 else tcol.at[core, 0, s],
              tcol.at[core, 0, s + 1], {"srow": r + 1})
        start((r > 0) & (r + s < nr), ("td", s + 1),
              t_ref.at[1] if s == 0 else tcol.at[core, 1, s],
              tcol.at[core, 1, s + 1], {"srow": r - 1})

    chain_x(0)
    for d in range(1, nc):
        start(True, ("xc", d), x_ref, xloc.at[nr + c], {"scol": lax.rem(c + d, nc)})
    chain_t(0)
    for d in range(1, nc):
        start(True, ("tc", d), t_ref, trow.at[core, c], {"scol": lax.rem(c + d, nc)})
    for copy in locals_t:
        copy.start()
    xloc[r] = x_ref[...]
    xloc[nr + c] = x_ref[...]
    for h in range(2):
        start(True, ("p", h, 0), t_ref.at[h], tcol.at[core, h, 0], mate)
    for s in range(1, nr):
        arrived(r >= s, ("xu", s), xloc.at[jnp.maximum(r - s, 0)])
        arrived(r + s < nr, ("xd", s), xloc.at[jnp.minimum(r + s, nr - 1)])
        if s < nr - 1:
            chain_x(s)
    for d in range(1, nc):
        arrived(True, ("xc", d), xloc.at[nr + lax.rem(c + nc - d, nc)])
    for d in range(1, nw):
        to = lax.rem(w + d, nw)
        start(True, ("xw", d), xloc.at[:, lax.rem(to, 2)], xg.at[w], {"win": to})
    own = pltpu.make_async_copy(xloc.at[:, core], xg.at[w], local.at[3])
    own.start()
    for d in range(1, nc):
        arrived(True, ("tc", d), trow.at[core, lax.rem(c + nc - d, nc)])
    for copy in locals_t:
        copy.wait()
    start(True, ("pr",), trow.at[core], trow.at[core], mate)
    for s in range(1, nr):
        arrived(r >= s, ("tu", s), tcol.at[core, 0, s])
        arrived(r + s < nr, ("td", s), tcol.at[core, 1, s])
        if s < nr - 1:
            chain_t(s)
        start(r >= s, ("p", 0, s), tcol.at[core, 0, s], tcol.at[core, 0, s], mate)
        start(r + s < nr, ("p", 1, s), tcol.at[core, 1, s], tcol.at[core, 1, s], mate)
    for d in range(1, nw):
        arrived(True, ("xw", d), xg.at[lax.rem(w + nw - d, nw)])
    own.wait()
    arrived(True, ("pr",), trow.at[1 - core])
    for s in range(nr):
        arrived(True if s == 0 else r >= s, ("p", 0, s), tcol.at[1 - core, 0, s])
        arrived(True if s == 0 else r + s < nr, ("p", 1, s), tcol.at[1 - core, 1, s])
    for cond, copy in pending:
        if cond is True:
            copy.wait_send()
        else:
            pl.when(cond)(copy.wait_send)


def exchange(x, t, nw, nr, nc):
    half_f, wl, n = x.shape[1], x.shape[3], x.shape[4]
    ph = t.shape[2]
    count = 4 * nr + 2 * nc + nw + 2 * nr + 2
    anywhere = pl.BlockSpec(memory_space=pl.ANY)
    return pl.pallas_call(
        functools.partial(exchange_kernel, nw, nr, nc),
        out_shape=(
            jax.ShapeDtypeStruct((nw, nr + nc, half_f, 2, wl, n), x.dtype),
            jax.ShapeDtypeStruct((2, 2, nr, n, ph), t.dtype),
            jax.ShapeDtypeStruct((2, nc, 2, n, ph), t.dtype),
        ),
        in_specs=[pl.BlockSpec(memory_space=pltpu.VMEM)] * 2,
        out_specs=(anywhere,) * 3,
        scratch_shapes=[
            pltpu.VMEM((nr + nc, 2, half_f, 2, wl, n), x.dtype),
            pltpu.SemaphoreType.DMA((count,)),
            pltpu.SemaphoreType.DMA((count,)),
            pltpu.SemaphoreType.DMA((4,)),
        ],
        compiler_params=pltpu.CompilerParams(collective_id=0, has_side_effects=True),
        name="exchange",
    )(x, t)


def beam_kernel(nr, nc, total, info, xrow, xcr, xci, tcol, trow, coh, part, kscr, csteer, rsteer):
    fi, t = pl.program_id(0), pl.program_id(1)
    r = info[0]
    scale = info[2 + fi].astype(jnp.float32) * (1.0 / NFFT)
    rows = xrow.shape[1]
    n, ph = tcol.shape[3], tcol.shape[4]
    step = 32

    @pl.when((fi == 0) & (t == 0))
    def _():
        part[...] = jnp.zeros_like(part)

    for slab in range(2):
        @pl.loop(0, n // step)
        def _(i):
            at = pl.ds(pl.multiple_of(i * step, step), step)
            cr, ci = steer(tcol[slab, 0, 0, at, :], scale)
            cr, ci = cr.astype(jnp.bfloat16), ci.astype(jnp.bfloat16)
            csteer[0, slab, at, :] = cr
            csteer[1, slab, at, :] = ci
            csteer[2, slab, at, :] = cr + ci

    @pl.when((t == 0) | (t == r + 1))
    def _():
        for slab in range(2):
            for block in range(nc):
                @pl.loop(0, n // step)
                def _(i):
                    at = pl.ds(pl.multiple_of(i * step, step), step)
                    to = pl.ds(pl.multiple_of(block * n + i * step, step), step)
                    rr, ri = steer(trow[slab, block, 0, at, :], scale)
                    rsteer[0, slab, to, :] = rr.astype(jnp.bfloat16).astype(jnp.float32)
                    rsteer[1, slab, to, :] = ri.astype(jnp.bfloat16).astype(jnp.float32)

    chunk = min(ROWS, rows)

    @pl.when(t != r + 1)
    def _():
        @pl.loop(0, rows // chunk)
        def _(m):
            at = pl.ds(pl.multiple_of(m * chunk, chunk), chunk)
            left = xrow[0, at, :]
            re = jnp.dot(left, xcr[0, 0], preferred_element_type=jnp.float32)
            im = jnp.dot(left, xci[0, 0], preferred_element_type=jnp.float32)
            inverse = lax.rsqrt(re * re + im * im + float(total))
            kr = (re * inverse).astype(jnp.bfloat16)
            ki = (im * inverse).astype(jnp.bfloat16)
            kscr[0, at, :] = kr
            kscr[1, at, :] = ki
            kscr[2, at, :] = kr + ki

            @pl.when(fi == 0)
            def _():
                coh[0, at, :] = kr
                coh[1, at, :] = ki

    half = jnp.where(t <= r, 0, 1)
    weight = jnp.where((t == r) | (t == r + 1), 1.0, 2.0)

    @pl.loop(0, rows // chunk)
    def _(m):
        at = pl.ds(pl.multiple_of(m * chunk, chunk), chunk)
        for slab in range(2):
            t1 = jnp.dot(kscr[0, at, :], csteer[0, slab], preferred_element_type=jnp.float32)
            t2 = jnp.dot(kscr[1, at, :], csteer[1, slab], preferred_element_type=jnp.float32)
            t3 = jnp.dot(kscr[2, at, :], csteer[2, slab], preferred_element_type=jnp.float32)
            v = rsteer[0, slab, at, :] * (t1 - t2) + rsteer[1, slab, at, :] * (t3 - (t1 + t2))
            v = jnp.sum(v.reshape(chunk // 8, 8, ph), axis=0)
            part[fi, half, slab] += weight * v


def beam_call(info, xrow, xcr, xci, tcol, trow, total):
    half_f, rows, depth = xrow.shape
    nr, n = xcr.shape[1], xcr.shape[3]
    nc, ph = trow.shape[1], trow.shape[4]

    def freq(fi, info):
        return lax.rem(info[1] + fi, half_f)

    def plane(t, info):
        return jnp.where(t <= info[0], t, t - 1)

    def col_map(fi, t, info):
        return (freq(fi, info), plane(t, info), 0, 0)

    def tcol_map(fi, t, info):
        r = info[0]
        return (0, jnp.where(t <= r, 0, 1), jnp.where(t <= r, r - t, t - 1 - r), 0, 0)

    def coh_map(fi, t, info):
        return (0, 0, jnp.where(fi == 0, plane(t, info), nr - 1))

    return pl.pallas_call(
        functools.partial(beam_kernel, nr, nc, total),
        out_shape=(
            jax.ShapeDtypeStruct((2, rows, nr * n), jnp.bfloat16),
            jax.ShapeDtypeStruct((half_f, 2, 2, 8, ph), jnp.float32),
        ),
        grid_spec=pltpu.PrefetchScalarGridSpec(
            num_scalar_prefetch=1,
            grid=(half_f, nr + 1),
            in_specs=[
                pl.BlockSpec((1, rows, depth), lambda fi, t, info: (freq(fi, info), 0, 0)),
                pl.BlockSpec((1, 1, depth, n), col_map),
                pl.BlockSpec((1, 1, depth, n), col_map),
                pl.BlockSpec((2, 1, 1, n, ph), tcol_map),
                pl.BlockSpec(
                    (2, nc, 1, n, ph),
                    lambda fi, t, info: (0, 0, jnp.where(t <= info[0], 0, 1), 0, 0),
                ),
            ],
            out_specs=(
                pl.BlockSpec((2, rows, n), coh_map),
                pl.BlockSpec((half_f, 2, 2, 8, ph), lambda fi, t, info: (0, 0, 0, 0, 0)),
            ),
            scratch_shapes=[
                pltpu.VMEM((3, rows, n), jnp.bfloat16),
                pltpu.VMEM((3, 2, n, ph), jnp.bfloat16),
                pltpu.VMEM((2, 2, rows, ph), jnp.float32),
            ],
        ),
        compiler_params=pltpu.CompilerParams(
            dimension_semantics=("arbitrary", "arbitrary"), vmem_limit_bytes=50 * 2**20
        ),
        name="beam",
    )(info, xrow, xcr, xci, tcol, trow)


def reduce_kernel(ng, nr, nc, stations, part_ref, beam_ref, held, send, recv):
    w, r, c = lax.axis_index("win"), lax.axis_index("srow"), lax.axis_index("scol")
    group, core, tile = w // 2, lax.rem(w, 2), r * nc + c
    tiles = nr * nc

    def place(fi, d, sign):
        to = lax.rem(tile + tiles + sign * d, tiles)
        return lax.rem(group + ng + sign * fi, ng), to

    def where(fi, d, sign):
        g, to = place(fi, d, sign)
        return {"win": 2 * g + core, "srow": to // nc, "scol": lax.rem(to, nc)}

    others = [(fi, d) for d in range(tiles) for fi in range(ng) if (fi, d) != (0, 0)]
    barrier = pltpu.get_barrier_semaphore()
    for fi, d in others:
        pl.semaphore_signal(barrier, inc=1, device_id=where(fi, d, 1), device_id_type=MESH)
    pl.semaphore_wait(barrier, len(others))

    def make(fi, d, dst):
        return pltpu.make_async_remote_copy(
            src_ref=part_ref.at[fi], dst_ref=dst, send_sem=send.at[fi, d], recv_sem=recv.at[fi, d],
            device_id=where(fi, d, 1), device_id_type=MESH,
        )

    sent = [make(fi, d, held.at[group, tile]) for fi, d in others]
    for copy in sent:
        copy.start()
    held[group, tile] = part_ref[0]
    for fi, d in others:
        g, to = place(fi, d, -1)
        make(fi, d, held.at[g, to]).wait_recv()
    beam_ref[...] = jnp.sum(held[...], axis=1) * (1.0 / stations)
    for copy in sent:
        copy.wait_send()


def reduce_beam(part, ng, nr, nc, stations):
    def kernel(*refs):
        reduce_kernel(ng, nr, nc, stations, *refs)

    return pl.pallas_call(
        kernel,
        out_shape=jax.ShapeDtypeStruct((ng,) + part.shape[1:], jnp.float32),
        in_specs=[pl.BlockSpec(memory_space=pltpu.VMEM)],
        out_specs=pl.BlockSpec(memory_space=pltpu.VMEM),
        scratch_shapes=[
            pltpu.VMEM((ng, nr * nc) + part.shape[1:], jnp.float32),
            pltpu.SemaphoreType.DMA((ng, nr * nc)),
            pltpu.SemaphoreType.DMA((ng, nr * nc)),
        ],
        compiler_params=pltpu.CompilerParams(collective_id=1, has_side_effects=True),
        name="reduce_beam",
    )(part)


def body(nw, nr, nc, spectra, bins, travel):
    w, r, c = lax.axis_index("win"), lax.axis_index("srow"), lax.axis_index("scol")
    group, core = w // 2, w % 2
    nf, _, wl, n = spectra.shape
    half_f = nf // 2
    ph = travel.shape[1] // 2
    x = phase_normalized(spectra).reshape(half_f, 2, 2, wl, n).swapaxes(0, 1)
    t = (travel % NFFT).astype(jnp.int16).reshape(n, 2, ph).swapaxes(0, 1)
    xg, tcol, trow = exchange(x, t, nw, nr, nc)
    cols = xg[:, :nr].transpose(2, 1, 3, 0, 4, 5)
    xcr = cols.reshape(half_f, nr, 2 * nw * wl, n)
    xci = jnp.stack([-cols[:, :, 1], cols[:, :, 0]], axis=2).reshape(half_f, nr, 2 * nw * wl, n)
    xrow = xg[:, nr:].transpose(2, 1, 5, 3, 0, 4).reshape(half_f, nc * n, 2 * nw * wl)
    info = jnp.concatenate([
        jnp.stack([r, group]).astype(jnp.int32),
        jnp.stack([bins[(group + i) % half_f * 2 + core] for i in range(half_f)]),
    ])
    coherent, part = beam_call(info, xrow, xcr, xci, tcol, trow, nw * wl)
    part = part.sum(axis=3).swapaxes(1, 2).reshape(half_f, 4 * ph // 128, 128)
    beam = reduce_beam(part, nw // 2, nr, nc, nr * nc * n).reshape(1, 2 * nw * ph)
    return coherent.reshape(1, 2, nc * n, nr, n), beam


def solution(mesh):
    sizes = [mesh.shape[a] for a in ("win", "srow", "scol")]
    placed = (P(None, None, "win", ("srow", "scol")), P(), P(("srow", "scol"), "win"))
    return jax.shard_map(
        functools.partial(body, *sizes),
        mesh=mesh,
        in_specs=placed,
        out_specs=(P("win", None, "srow", None, "scol"), P("win", None)),
        check_vma=False,
    )
```

```python
import functools
import math

import jax
import jax.numpy as jnp
import numpy as np
from jax import lax
from jax.experimental import pallas as pl
from jax.experimental.pallas import tpu as pltpu
from jax.sharding import PartitionSpec as P

NFFT = 4096
MESH = pl.DeviceIdType.MESH
MAGIC = 12582912.0
ROWS = 512
BEAM_ROWS = 1024


def phase_normalized(spectra):
    magnitude = jnp.sqrt(spectra[:, 0] * spectra[:, 0] + spectra[:, 1] * spectra[:, 1] + 0.5)
    return (spectra / magnitude[:, None]).astype(jnp.bfloat16)


def fitted():
    nodes = 0.25 * (1.0 - np.cos(np.pi * (np.arange(64) + 0.5) / 64)) / 2.0
    root = np.sqrt(nodes)
    powers = np.vander(nodes, 5, increasing=True)
    sine = np.linalg.lstsq(powers, np.sin(np.pi * root) / root, rcond=None)[0]
    cosine = np.linalg.lstsq(powers, -2.0 * np.cos(np.pi * root), rcond=None)[0]
    return [float(a) for a in sine], [float(a) for a in cosine]


def steer(travel, scale):
    sine, cosine = fitted()
    turns = travel.astype(jnp.int32).astype(jnp.float32) * scale
    rest = turns - ((turns + MAGIC) - MAGIC)
    z = rest * rest
    s = sine[4]
    c = cosine[4]
    for k in (3, 2, 1, 0):
        s = s * z + sine[k]
        c = c * z + cosine[k]
    s = s * rest
    return 1.0 - 2.0 * (s * s), s * c


def exchange_kernel(nw, nr, nc, x_ref, t_ref, xg, tcol, trow, xloc, send, recv, local):
    w, r, c = lax.axis_index("win"), lax.axis_index("srow"), lax.axis_index("scol")
    core = lax.rem(w, 2)
    mate = {"win": w + 1 - 2 * core}
    number = {}

    def slot(*name):
        return number.setdefault(name, len(number))

    def make(name, src, dst, where):
        k = slot(*name)
        return pltpu.make_async_remote_copy(
            src_ref=src, dst_ref=dst, send_sem=send.at[k], recv_sem=recv.at[k],
            device_id=where, device_id_type=MESH,
        )

    pending = []

    def start(cond, name, src, dst, where):
        copy = make(name, src, dst, where)
        if cond is True:
            copy.start()
        else:
            pl.when(cond)(copy.start)
        pending.append((cond, copy))

    def arrived(cond, name, dst):
        copy = make(name, dst, dst, mate)
        if cond is True:
            copy.wait_recv()
        else:
            pl.when(cond)(copy.wait_recv)

    barrier = pltpu.get_barrier_semaphore()

    def greet(where):
        pl.semaphore_signal(barrier, inc=1, device_id=where, device_id_type=MESH)

    pl.when(r > 0)(lambda: greet({"srow": r - 1}))
    pl.when(r < nr - 1)(lambda: greet({"srow": r + 1}))
    for d in range(1, nc):
        greet({"scol": lax.rem(c + d, nc)})
    for d in range(1, nw):
        greet({"win": lax.rem(w + d, nw)})
    ends = jnp.where(r > 0, 1, 0) + jnp.where(r < nr - 1, 1, 0)
    pl.semaphore_wait(barrier, ends + nc - 1 + nw - 1)

    locals_t = [
        pltpu.make_async_copy(t_ref.at[0], tcol.at[core, 0, 0], local.at[0]),
        pltpu.make_async_copy(t_ref.at[1], tcol.at[core, 1, 0], local.at[1]),
        pltpu.make_async_copy(t_ref, trow.at[core, c], local.at[2]),
    ]

    def chain_x(s):
        start((r < nr - 1) & (r >= s), ("xu", s + 1),
              x_ref if s == 0 else xloc.at[jnp.maximum(r - s, 0)],
              xloc.at[jnp.maximum(r - s, 0)], {"srow": r + 1})
        start((r > 0) & (r + s < nr), ("xd", s + 1),
              x_ref if s == 0 else xloc.at[jnp.minimum(r + s, nr - 1)],
              xloc.at[jnp.minimum(r + s, nr - 1)], {"srow": r - 1})

    def chain_t(s):
        start((r < nr - 1) & (r >= s), ("tu", s + 1),
              t_ref.at[0] if s == 0 else tcol.at[core, 0, s],
              tcol.at[core, 0, s + 1], {"srow": r + 1})
        start((r > 0) & (r + s < nr), ("td", s + 1),
              t_ref.at[1] if s == 0 else tcol.at[core, 1, s],
              tcol.at[core, 1, s + 1], {"srow": r - 1})

    chain_x(0)
    for d in range(1, nc):
        start(True, ("xc", d), x_ref, xloc.at[nr + c], {"scol": lax.rem(c + d, nc)})
    chain_t(0)
    for d in range(1, nc):
        start(True, ("tc", d), t_ref, trow.at[core, c], {"scol": lax.rem(c + d, nc)})
    for copy in locals_t:
        copy.start()
    xloc[r] = x_ref[...]
    xloc[nr + c] = x_ref[...]
    for h in range(2):
        start(True, ("p", h, 0), t_ref.at[h], tcol.at[core, h, 0], mate)
    for s in range(1, nr):
        arrived(r >= s, ("xu", s), xloc.at[jnp.maximum(r - s, 0)])
        arrived(r + s < nr, ("xd", s), xloc.at[jnp.minimum(r + s, nr - 1)])
        if s < nr - 1:
            chain_x(s)
    for d in range(1, nc):
        arrived(True, ("xc", d), xloc.at[nr + lax.rem(c + nc - d, nc)])
    for d in range(1, nw):
        to = lax.rem(w + d, nw)
        start(True, ("xw", d), xloc.at[:, lax.rem(to, 2)], xg.at[w], {"win": to})
    own = pltpu.make_async_copy(xloc.at[:, core], xg.at[w], local.at[3])
    own.start()
    for d in range(1, nc):
        arrived(True, ("tc", d), trow.at[core, lax.rem(c + nc - d, nc)])
    for copy in locals_t:
        copy.wait()
    start(True, ("pr",), trow.at[core], trow.at[core], mate)
    for s in range(1, nr):
        arrived(r >= s, ("tu", s), tcol.at[core, 0, s])
        arrived(r + s < nr, ("td", s), tcol.at[core, 1, s])
        if s < nr - 1:
            chain_t(s)
        start(r >= s, ("p", 0, s), tcol.at[core, 0, s], tcol.at[core, 0, s], mate)
        start(r + s < nr, ("p", 1, s), tcol.at[core, 1, s], tcol.at[core, 1, s], mate)
    for d in range(1, nw):
        arrived(True, ("xw", d), xg.at[lax.rem(w + nw - d, nw)])
    own.wait()
    arrived(True, ("pr",), trow.at[1 - core])
    for s in range(nr):
        arrived(True if s == 0 else r >= s, ("p", 0, s), tcol.at[1 - core, 0, s])
        arrived(True if s == 0 else r + s < nr, ("p", 1, s), tcol.at[1 - core, 1, s])
    for cond, copy in pending:
        if cond is True:
            copy.wait_send()
        else:
            pl.when(cond)(copy.wait_send)


def exchange(x, t, nw, nr, nc):
    half_f, wl, n = x.shape[1], x.shape[3], x.shape[4]
    ph = t.shape[2]
    count = 4 * nr + 2 * nc + nw + 2 * nr + 2
    anywhere = pl.BlockSpec(memory_space=pl.ANY)
    return pl.pallas_call(
        functools.partial(exchange_kernel, nw, nr, nc),
        out_shape=(
            jax.ShapeDtypeStruct((nw, nr + nc, half_f, 2, wl, n), x.dtype),
            jax.ShapeDtypeStruct((2, 2, nr, n, ph), t.dtype),
            jax.ShapeDtypeStruct((2, nc, 2, n, ph), t.dtype),
        ),
        in_specs=[pl.BlockSpec(memory_space=pltpu.VMEM)] * 2,
        out_specs=(anywhere,) * 3,
        scratch_shapes=[
            pltpu.VMEM((nr + nc, 2, half_f, 2, wl, n), x.dtype),
            pltpu.SemaphoreType.DMA((count,)),
            pltpu.SemaphoreType.DMA((count,)),
            pltpu.SemaphoreType.DMA((4,)),
        ],
        compiler_params=pltpu.CompilerParams(collective_id=0, has_side_effects=True),
        name="exchange",
    )(x, t)


def beam_kernel(nr, nc, total, info, xrow, xcr, xci, tcol, trow, coh, part, kscr, csteer, rsteer):
    fi, t = pl.program_id(0), pl.program_id(1)
    r = info[0]
    scale = info[2 + fi].astype(jnp.float32) * (1.0 / NFFT)
    rows = xrow.shape[1]
    n, ph = tcol.shape[3], tcol.shape[4]
    step = 64
    halves = [pl.ds(slab * ph, ph) for slab in range(2)]

    @pl.when((fi == 0) & (t == 0))
    def _():
        part[...] = jnp.zeros_like(part)

    @pl.when((t == 0) | (t == r + 1))
    def _():
        for slab in range(2):
            for block in range(nc):
                @pl.loop(0, n // step)
                def _(i):
                    at = pl.ds(pl.multiple_of(i * step, step), step)
                    to = pl.ds(pl.multiple_of(block * n + i * step, step), step)
                    rr, ri = steer(trow[slab, block, 0, at, :], scale)
                    rsteer[0, to, halves[slab]] = rr.astype(jnp.bfloat16).astype(jnp.float32)
                    rsteer[1, to, halves[slab]] = ri.astype(jnp.bfloat16).astype(jnp.float32)

    own = (t == r) | (t == r + 1)

    @pl.when(own)
    def _():
        @pl.loop(0, n // step)
        def _(i):
            at = pl.ds(pl.multiple_of(i * step, step), step)
            come = pl.ds(pl.multiple_of(info[2 + part.shape[0]] * n + i * step, step), step)
            cr = rsteer[0, come, :].astype(jnp.bfloat16)
            ci = rsteer[1, come, :].astype(jnp.bfloat16)
            csteer[0, at, :] = cr
            csteer[1, at, :] = ci
            csteer[2, at, :] = cr + ci

    @pl.when(jnp.logical_not(own))
    def _():
        for slab in range(2):
            @pl.loop(0, n // step)
            def _(i):
                at = pl.ds(pl.multiple_of(i * step, step), step)
                side = halves[slab]
                cr, ci = steer(tcol[slab, 0, 0, at, :], scale)
                cr, ci = cr.astype(jnp.bfloat16), ci.astype(jnp.bfloat16)
                csteer[0, at, side] = cr
                csteer[1, at, side] = ci
                csteer[2, at, side] = cr + ci

    chunk = min(ROWS, rows)

    @pl.when(t != r + 1)
    def _():
        @pl.loop(0, rows // chunk)
        def _(m):
            at = pl.ds(pl.multiple_of(m * chunk, chunk), chunk)
            left = xrow[0, at, :]
            re = jnp.dot(left, xcr[0, 0], preferred_element_type=jnp.float32)
            im = jnp.dot(left, xci[0, 0], preferred_element_type=jnp.float32)
            inverse = lax.rsqrt(re * re + im * im + float(total))
            kr = (re * inverse).astype(jnp.bfloat16)
            ki = (im * inverse).astype(jnp.bfloat16)
            kscr[0, at, :] = kr
            kscr[1, at, :] = ki
            kscr[2, at, :] = kr + ki

            @pl.when(fi == 0)
            def _():
                coh[0, at, :] = kr
                coh[1, at, :] = ki

    half = jnp.where(t <= r, 0, 1)
    weight = jnp.where(own, 1.0, 2.0)

    chunk = min(BEAM_ROWS, rows)

    @pl.loop(0, rows // chunk)
    def _(m):
        at = pl.ds(pl.multiple_of(m * chunk, chunk), chunk)
        for side in halves:
            t1 = jnp.dot(kscr[0, at, :], csteer[0, :, side], preferred_element_type=jnp.float32)
            t2 = jnp.dot(kscr[1, at, :], csteer[1, :, side], preferred_element_type=jnp.float32)
            t3 = jnp.dot(kscr[2, at, :], csteer[2, :, side], preferred_element_type=jnp.float32)
            v = rsteer[0, at, side] * (t1 - t2) + rsteer[1, at, side] * (t3 - (t1 + t2))
            v = jnp.sum(v.reshape(chunk // 8, 8, v.shape[1]), axis=0)
            part[fi, half, :, side] += weight * v


def beam_call(info, xrow, xcr, xci, tcol, trow, total):
    half_f, rows, depth = xrow.shape
    nr, n = xcr.shape[1], xcr.shape[3]
    nc, ph = trow.shape[1], trow.shape[4]

    def freq(fi, info):
        return lax.rem(info[1] + fi, half_f)

    def plane(t, info):
        return jnp.where(t <= info[0], t, t - 1)

    def col_map(fi, t, info):
        return (freq(fi, info), plane(t, info), 0, 0)

    def tcol_map(fi, t, info):
        r = info[0]
        return (0, jnp.where(t <= r, 0, 1), jnp.where(t <= r, r - t, t - 1 - r), 0, 0)

    def coh_map(fi, t, info):
        return (0, 0, jnp.where(fi == 0, plane(t, info), nr - 1))

    return pl.pallas_call(
        functools.partial(beam_kernel, nr, nc, total),
        out_shape=(
            jax.ShapeDtypeStruct((2, rows, nr * n), jnp.bfloat16),
            jax.ShapeDtypeStruct((half_f, 2, 8, 2 * ph), jnp.float32),
        ),
        grid_spec=pltpu.PrefetchScalarGridSpec(
            num_scalar_prefetch=1,
            grid=(half_f, nr + 1),
            in_specs=[
                pl.BlockSpec((1, rows, depth), lambda fi, t, info: (freq(fi, info), 0, 0)),
                pl.BlockSpec((1, 1, depth, n), col_map),
                pl.BlockSpec((1, 1, depth, n), col_map),
                pl.BlockSpec((2, 1, 1, n, ph), tcol_map),
                pl.BlockSpec(
                    (2, nc, 1, n, ph),
                    lambda fi, t, info: (0, 0, jnp.where(t <= info[0], 0, 1), 0, 0),
                ),
            ],
            out_specs=(
                pl.BlockSpec((2, rows, n), coh_map),
                pl.BlockSpec((half_f, 2, 8, 2 * ph), lambda fi, t, info: (0, 0, 0, 0)),
            ),
            scratch_shapes=[
                pltpu.VMEM((3, rows, n), jnp.bfloat16),
                pltpu.VMEM((3, n, 2 * ph), jnp.bfloat16),
                pltpu.VMEM((2, rows, 2 * ph), jnp.float32),
            ],
        ),
        compiler_params=pltpu.CompilerParams(
            dimension_semantics=("arbitrary", "arbitrary"), vmem_limit_bytes=50 * 2**20
        ),
        name="beam",
    )(info, xrow, xcr, xci, tcol, trow)


def reduce_kernel(ng, nr, nc, stations, part_ref, beam_ref, held, send, recv):
    w, r, c = lax.axis_index("win"), lax.axis_index("srow"), lax.axis_index("scol")
    group, core, tile = w // 2, lax.rem(w, 2), r * nc + c
    tiles = nr * nc

    def place(fi, d, sign):
        to = lax.rem(tile + tiles + sign * d, tiles)
        return lax.rem(group + ng + sign * fi, ng), to

    def where(fi, d, sign):
        g, to = place(fi, d, sign)
        return {"win": 2 * g + core, "srow": to // nc, "scol": lax.rem(to, nc)}

    others = [(fi, d) for d in range(tiles) for fi in range(ng) if (fi, d) != (0, 0)]
    barrier = pltpu.get_barrier_semaphore()
    for fi, d in others:
        pl.semaphore_signal(barrier, inc=1, device_id=where(fi, d, 1), device_id_type=MESH)
    pl.semaphore_wait(barrier, len(others))

    def make(fi, d, dst):
        return pltpu.make_async_remote_copy(
            src_ref=part_ref.at[fi], dst_ref=dst, send_sem=send.at[fi, d], recv_sem=recv.at[fi, d],
            device_id=where(fi, d, 1), device_id_type=MESH,
        )

    sent = [make(fi, d, held.at[group, tile]) for fi, d in others]
    for copy in sent:
        copy.start()
    held[group, tile] = part_ref[0]
    for fi, d in others:
        g, to = place(fi, d, -1)
        make(fi, d, held.at[g, to]).wait_recv()
    beam_ref[...] = jnp.sum(held[...], axis=1) * (1.0 / stations)
    for copy in sent:
        copy.wait_send()


def reduce_beam(part, ng, nr, nc, stations):
    def kernel(*refs):
        reduce_kernel(ng, nr, nc, stations, *refs)

    return pl.pallas_call(
        kernel,
        out_shape=jax.ShapeDtypeStruct((ng,) + part.shape[1:], jnp.float32),
        in_specs=[pl.BlockSpec(memory_space=pltpu.VMEM)],
        out_specs=pl.BlockSpec(memory_space=pltpu.VMEM),
        scratch_shapes=[
            pltpu.VMEM((ng, nr * nc) + part.shape[1:], jnp.float32),
            pltpu.SemaphoreType.DMA((ng, nr * nc)),
            pltpu.SemaphoreType.DMA((ng, nr * nc)),
        ],
        compiler_params=pltpu.CompilerParams(collective_id=1, has_side_effects=True),
        name="reduce_beam",
    )(part)


def body(nw, nr, nc, spectra, bins, travel):
    w, r, c = lax.axis_index("win"), lax.axis_index("srow"), lax.axis_index("scol")
    group, core = w // 2, w % 2
    nf, _, wl, n = spectra.shape
    half_f = nf // 2
    ph = travel.shape[1] // 2
    x = phase_normalized(spectra).reshape(half_f, 2, 2, wl, n).swapaxes(0, 1)
    t = (travel % NFFT).astype(jnp.int16).reshape(n, 2, ph).swapaxes(0, 1)
    xg, tcol, trow = exchange(x, t, nw, nr, nc)
    cols = xg[:, :nr].transpose(2, 1, 3, 0, 4, 5)
    xcr = cols.reshape(half_f, nr, 2 * nw * wl, n)
    xci = jnp.stack([-cols[:, :, 1], cols[:, :, 0]], axis=2).reshape(half_f, nr, 2 * nw * wl, n)
    xrow = xg[:, nr:].transpose(2, 1, 5, 3, 0, 4).reshape(half_f, nc * n, 2 * nw * wl)
    info = jnp.concatenate([
        jnp.stack([r, group]).astype(jnp.int32),
        jnp.stack([bins[(group + i) % half_f * 2 + core] for i in range(half_f)]),
        c[None].astype(jnp.int32),
    ])
    coherent, part = beam_call(info, xrow, xcr, xci, tcol, trow, nw * wl)
    part = part.sum(axis=2).reshape(half_f, 2, 2, ph).swapaxes(1, 2).reshape(half_f, 4 * ph // 128, 128)
    beam = reduce_beam(part, nw // 2, nr, nc, nr * nc * n).reshape(1, 2 * nw * ph)
    return coherent.reshape(1, 2, nc * n, nr, n), beam


def solution(mesh):
    sizes = [mesh.shape[a] for a in ("win", "srow", "scol")]
    placed = (P(None, None, "win", ("srow", "scol")), P(), P(("srow", "scol"), "win"))
    return jax.shard_map(
        functools.partial(body, *sizes),
        mesh=mesh,
        in_specs=placed,
        out_specs=(P("win", None, "srow", None, "scol"), P("win", None)),
        check_vma=False,
    )
```

```python
import functools
import math

import jax
import jax.numpy as jnp
import numpy as np
from jax import lax
from jax.experimental import pallas as pl
from jax.experimental.pallas import tpu as pltpu
from jax.sharding import PartitionSpec as P

NFFT = 4096
MESH = pl.DeviceIdType.MESH
MAGIC = 12582912.0
ROWS = 512
BEAM_ROWS = 1024


def phase_normalized(spectra):
    magnitude = jnp.sqrt(spectra[:, 0] * spectra[:, 0] + spectra[:, 1] * spectra[:, 1] + 0.5)
    return (spectra / magnitude[:, None]).astype(jnp.bfloat16)


def fitted():
    nodes = 0.25 * (1.0 - np.cos(np.pi * (np.arange(64) + 0.5) / 64)) / 2.0
    root = np.sqrt(nodes)
    powers = np.vander(nodes, 5, increasing=True)
    sine = np.linalg.lstsq(powers, np.sin(np.pi * root) / root, rcond=None)[0]
    cosine = np.linalg.lstsq(powers, -2.0 * np.cos(np.pi * root), rcond=None)[0]
    return [float(a) for a in sine], [float(a) for a in cosine]


def steer(travel, scale):
    sine, cosine = fitted()
    turns = travel.astype(jnp.int32).astype(jnp.float32) * scale
    rest = turns - ((turns + MAGIC) - MAGIC)
    z = rest * rest
    s = sine[4]
    c = cosine[4]
    for k in (3, 2, 1, 0):
        s = s * z + sine[k]
        c = c * z + cosine[k]
    s = s * rest
    return 1.0 - 2.0 * (s * s), s * c


def exchange_kernel(nw, nr, nc, x_ref, t_ref, xg, tcol, trow, xloc, send, recv, local):
    w, r, c = lax.axis_index("win"), lax.axis_index("srow"), lax.axis_index("scol")
    core = lax.rem(w, 2)
    mate = {"win": w + 1 - 2 * core}
    number = {}

    def slot(*name):
        return number.setdefault(name, len(number))

    def make(name, src, dst, where):
        k = slot(*name)
        return pltpu.make_async_remote_copy(
            src_ref=src, dst_ref=dst, send_sem=send.at[k], recv_sem=recv.at[k],
            device_id=where, device_id_type=MESH,
        )

    pending = []

    def start(cond, name, src, dst, where):
        copy = make(name, src, dst, where)
        if cond is True:
            copy.start()
        else:
            pl.when(cond)(copy.start)
        pending.append((cond, copy))

    def arrived(cond, name, dst):
        copy = make(name, dst, dst, mate)
        if cond is True:
            copy.wait_recv()
        else:
            pl.when(cond)(copy.wait_recv)

    barrier = pltpu.get_barrier_semaphore()

    def greet(where):
        pl.semaphore_signal(barrier, inc=1, device_id=where, device_id_type=MESH)

    pl.when(r > 0)(lambda: greet({"srow": r - 1}))
    pl.when(r < nr - 1)(lambda: greet({"srow": r + 1}))
    for d in range(1, nc):
        greet({"scol": lax.rem(c + d, nc)})
    for d in range(1, nw):
        greet({"win": lax.rem(w + d, nw)})
    ends = jnp.where(r > 0, 1, 0) + jnp.where(r < nr - 1, 1, 0)
    pl.semaphore_wait(barrier, ends + nc - 1 + nw - 1)

    locals_t = [
        pltpu.make_async_copy(t_ref.at[0], tcol.at[core, 0, 0], local.at[0]),
        pltpu.make_async_copy(t_ref.at[1], tcol.at[core, 1, 0], local.at[1]),
        pltpu.make_async_copy(t_ref, trow.at[core, c], local.at[2]),
    ]

    def chain_x(s):
        start((r < nr - 1) & (r >= s), ("xu", s + 1),
              x_ref if s == 0 else xloc.at[jnp.maximum(r - s, 0)],
              xloc.at[jnp.maximum(r - s, 0)], {"srow": r + 1})
        start((r > 0) & (r + s < nr), ("xd", s + 1),
              x_ref if s == 0 else xloc.at[jnp.minimum(r + s, nr - 1)],
              xloc.at[jnp.minimum(r + s, nr - 1)], {"srow": r - 1})

    def chain_t(s):
        start((r < nr - 1) & (r >= s), ("tu", s + 1),
              t_ref.at[0] if s == 0 else tcol.at[core, 0, s],
              tcol.at[core, 0, s + 1], {"srow": r + 1})
        start((r > 0) & (r + s < nr), ("td", s + 1),
              t_ref.at[1] if s == 0 else tcol.at[core, 1, s],
              tcol.at[core, 1, s + 1], {"srow": r - 1})

    chain_x(0)
    for d in range(1, nc):
        start(True, ("xc", d), x_ref, xloc.at[nr + c], {"scol": lax.rem(c + d, nc)})
    chain_t(0)
    for d in range(1, nc):
        start(True, ("tc", d), t_ref, trow.at[core, c], {"scol": lax.rem(c + d, nc)})
    for copy in locals_t:
        copy.start()
    xloc[r] = x_ref[...]
    xloc[nr + c] = x_ref[...]
    for h in range(2):
        start(True, ("p", h, 0), t_ref.at[h], tcol.at[core, h, 0], mate)
    for s in range(1, nr):
        arrived(r >= s, ("xu", s), xloc.at[jnp.maximum(r - s, 0)])
        arrived(r + s < nr, ("xd", s), xloc.at[jnp.minimum(r + s, nr - 1)])
        if s < nr - 1:
            chain_x(s)
    for d in range(1, nc):
        arrived(True, ("xc", d), xloc.at[nr + lax.rem(c + nc - d, nc)])
    for d in range(1, nw):
        to = lax.rem(w + d, nw)
        start(True, ("xw", d), xloc.at[:, lax.rem(to, 2)], xg.at[w], {"win": to})
    own = pltpu.make_async_copy(xloc.at[:, core], xg.at[w], local.at[3])
    own.start()
    for d in range(1, nc):
        arrived(True, ("tc", d), trow.at[core, lax.rem(c + nc - d, nc)])
    for copy in locals_t:
        copy.wait()
    start(True, ("pr",), trow.at[core], trow.at[core], mate)
    for s in range(1, nr):
        arrived(r >= s, ("tu", s), tcol.at[core, 0, s])
        arrived(r + s < nr, ("td", s), tcol.at[core, 1, s])
        if s < nr - 1:
            chain_t(s)
        start(r >= s, ("p", 0, s), tcol.at[core, 0, s], tcol.at[core, 0, s], mate)
        start(r + s < nr, ("p", 1, s), tcol.at[core, 1, s], tcol.at[core, 1, s], mate)
    for d in range(1, nw):
        arrived(True, ("xw", d), xg.at[lax.rem(w + nw - d, nw)])
    own.wait()
    arrived(True, ("pr",), trow.at[1 - core])
    for s in range(nr):
        arrived(True if s == 0 else r >= s, ("p", 0, s), tcol.at[1 - core, 0, s])
        arrived(True if s == 0 else r + s < nr, ("p", 1, s), tcol.at[1 - core, 1, s])
    for cond, copy in pending:
        if cond is True:
            copy.wait_send()
        else:
            pl.when(cond)(copy.wait_send)


def exchange(x, t, nw, nr, nc):
    half_f, wl, n = x.shape[1], x.shape[3], x.shape[4]
    ph = t.shape[2]
    count = 4 * nr + 2 * nc + nw + 2 * nr + 2
    anywhere = pl.BlockSpec(memory_space=pl.ANY)
    return pl.pallas_call(
        functools.partial(exchange_kernel, nw, nr, nc),
        out_shape=(
            jax.ShapeDtypeStruct((nw, nr + nc, half_f, 2, wl, n), x.dtype),
            jax.ShapeDtypeStruct((2, 2, nr, n, ph), t.dtype),
            jax.ShapeDtypeStruct((2, nc, 2, n, ph), t.dtype),
        ),
        in_specs=[pl.BlockSpec(memory_space=pltpu.VMEM)] * 2,
        out_specs=(anywhere,) * 3,
        scratch_shapes=[
            pltpu.VMEM((nr + nc, 2, half_f, 2, wl, n), x.dtype),
            pltpu.SemaphoreType.DMA((count,)),
            pltpu.SemaphoreType.DMA((count,)),
            pltpu.SemaphoreType.DMA((4,)),
        ],
        compiler_params=pltpu.CompilerParams(collective_id=0, has_side_effects=True),
        name="exchange",
    )(x, t)


def beam_kernel(nr, nc, total, info, xrow, xcr, xci, tcol, trow, coh, part, kscr, csteer, rsteer):
    fi, t = pl.program_id(0), pl.program_id(1)
    r = info[0]
    scale = info[2 + fi].astype(jnp.float32) * (1.0 / NFFT)
    rows = xrow.shape[1]
    n, ph = tcol.shape[3], tcol.shape[4]
    step = 64
    halves = [pl.ds(slab * ph, ph) for slab in range(2)]

    @pl.when((fi == 0) & (t == 0))
    def _():
        part[...] = jnp.zeros_like(part)

    @pl.when((t == 0) | (t == r + 1))
    def _():
        for slab in range(2):
            for block in range(nc):
                @pl.loop(0, n // step)
                def _(i):
                    at = pl.ds(pl.multiple_of(i * step, step), step)
                    to = pl.ds(pl.multiple_of(block * n + i * step, step), step)
                    rr, ri = steer(trow[slab, block, 0, at, :], scale)
                    rsteer[0, to, halves[slab]] = rr.astype(jnp.bfloat16).astype(jnp.float32)
                    rsteer[1, to, halves[slab]] = ri.astype(jnp.bfloat16).astype(jnp.float32)

    own = (t == r) | (t == r + 1)

    @pl.when(own)
    def _():
        @pl.loop(0, n // step)
        def _(i):
            at = pl.ds(pl.multiple_of(i * step, step), step)
            come = pl.ds(pl.multiple_of(info[2 + part.shape[0]] * n + i * step, step), step)
            cr = rsteer[0, come, :].astype(jnp.bfloat16)
            ci = rsteer[1, come, :].astype(jnp.bfloat16)
            csteer[0, at, :] = cr
            csteer[1, at, :] = ci
            csteer[2, at, :] = cr + ci

    @pl.when(jnp.logical_not(own))
    def _():
        for slab in range(2):
            @pl.loop(0, n // step)
            def _(i):
                at = pl.ds(pl.multiple_of(i * step, step), step)
                side = halves[slab]
                cr, ci = steer(tcol[slab, 0, 0, at, :], scale)
                cr, ci = cr.astype(jnp.bfloat16), ci.astype(jnp.bfloat16)
                csteer[0, at, side] = cr
                csteer[1, at, side] = ci
                csteer[2, at, side] = cr + ci

    chunk = min(ROWS, rows)

    @pl.when(t != r + 1)
    def _():
        @pl.loop(0, rows // chunk)
        def _(m):
            at = pl.ds(pl.multiple_of(m * chunk, chunk), chunk)
            left = xrow[0, at, :]
            re = jnp.dot(left, xcr[0, 0], preferred_element_type=jnp.float32)
            im = jnp.dot(left, xci[0, 0], preferred_element_type=jnp.float32)
            inverse = lax.rsqrt(re * re + im * im + float(total))
            kr = (re * inverse).astype(jnp.bfloat16)
            ki = (im * inverse).astype(jnp.bfloat16)
            kscr[0, at, :] = kr
            kscr[1, at, :] = ki
            kscr[2, at, :] = kr + ki

            @pl.when(fi == 0)
            def _():
                coh[0, 0, at, :] = kr
                coh[1, 0, at, :] = ki

    half = jnp.where(t <= r, 0, 1)
    weight = jnp.where(own, 1.0, 2.0)

    chunk = min(BEAM_ROWS, rows)

    @pl.loop(0, rows // chunk)
    def _(m):
        at = pl.ds(pl.multiple_of(m * chunk, chunk), chunk)
        for side in halves:
            t1 = jnp.dot(kscr[0, at, :], csteer[0, :, side], preferred_element_type=jnp.float32)
            t2 = jnp.dot(kscr[1, at, :], csteer[1, :, side], preferred_element_type=jnp.float32)
            t3 = jnp.dot(kscr[2, at, :], csteer[2, :, side], preferred_element_type=jnp.float32)
            v = rsteer[0, at, side] * (t1 - t2) + rsteer[1, at, side] * (t3 - (t1 + t2))
            v = jnp.sum(v.reshape(chunk // 8, 8, v.shape[1]), axis=0)
            part[fi, half, :, side] += weight * v


def beam_call(info, xrow, xcr, xci, tcol, trow, total):
    half_f, rows, depth = xrow.shape
    nr, n = xcr.shape[1], xcr.shape[3]
    nc, ph = trow.shape[1], trow.shape[4]

    def freq(fi, info):
        return lax.rem(info[1] + fi, half_f)

    def plane(t, info):
        return jnp.where(t <= info[0], t, t - 1)

    def col_map(fi, t, info):
        return (freq(fi, info), plane(t, info), 0, 0)

    def tcol_map(fi, t, info):
        r = info[0]
        return (0, jnp.where(t <= r, 0, 1), jnp.where(t <= r, r - t, t - 1 - r), 0, 0)

    def coh_map(fi, t, info):
        return (0, jnp.where(fi == 0, plane(t, info), nr - 1), 0, 0)

    return pl.pallas_call(
        functools.partial(beam_kernel, nr, nc, total),
        out_shape=(
            jax.ShapeDtypeStruct((2, nr, rows, n), jnp.bfloat16),
            jax.ShapeDtypeStruct((half_f, 2, 8, 2 * ph), jnp.float32),
        ),
        grid_spec=pltpu.PrefetchScalarGridSpec(
            num_scalar_prefetch=1,
            grid=(half_f, nr + 1),
            in_specs=[
                pl.BlockSpec((1, rows, depth), lambda fi, t, info: (freq(fi, info), 0, 0)),
                pl.BlockSpec((1, 1, depth, n), col_map),
                pl.BlockSpec((1, 1, depth, n), col_map),
                pl.BlockSpec((2, 1, 1, n, ph), tcol_map),
                pl.BlockSpec(
                    (2, nc, 1, n, ph),
                    lambda fi, t, info: (0, 0, jnp.where(t <= info[0], 0, 1), 0, 0),
                ),
            ],
            out_specs=(
                pl.BlockSpec((2, 1, rows, n), coh_map),
                pl.BlockSpec((half_f, 2, 8, 2 * ph), lambda fi, t, info: (0, 0, 0, 0)),
            ),
            scratch_shapes=[
                pltpu.VMEM((3, rows, n), jnp.bfloat16),
                pltpu.VMEM((3, n, 2 * ph), jnp.bfloat16),
                pltpu.VMEM((2, rows, 2 * ph), jnp.float32),
            ],
        ),
        compiler_params=pltpu.CompilerParams(
            dimension_semantics=("arbitrary", "arbitrary"), vmem_limit_bytes=50 * 2**20
        ),
        name="beam",
    )(info, xrow, xcr, xci, tcol, trow)


def reduce_kernel(ng, nr, nc, stations, part_ref, beam_ref, held, send, recv):
    w, r, c = lax.axis_index("win"), lax.axis_index("srow"), lax.axis_index("scol")
    group, core, tile = w // 2, lax.rem(w, 2), r * nc + c
    tiles = nr * nc

    def place(fi, d, sign):
        to = lax.rem(tile + tiles + sign * d, tiles)
        return lax.rem(group + ng + sign * fi, ng), to

    def where(fi, d, sign):
        g, to = place(fi, d, sign)
        return {"win": 2 * g + core, "srow": to // nc, "scol": lax.rem(to, nc)}

    others = [(fi, d) for d in range(tiles) for fi in range(ng) if (fi, d) != (0, 0)]
    barrier = pltpu.get_barrier_semaphore()
    for fi, d in others:
        pl.semaphore_signal(barrier, inc=1, device_id=where(fi, d, 1), device_id_type=MESH)
    pl.semaphore_wait(barrier, len(others))

    def make(fi, d, dst):
        return pltpu.make_async_remote_copy(
            src_ref=part_ref.at[fi], dst_ref=dst, send_sem=send.at[fi, d], recv_sem=recv.at[fi, d],
            device_id=where(fi, d, 1), device_id_type=MESH,
        )

    sent = [make(fi, d, held.at[group, tile]) for fi, d in others]
    for copy in sent:
        copy.start()
    held[group, tile] = part_ref[0]
    for fi, d in others:
        g, to = place(fi, d, -1)
        make(fi, d, held.at[g, to]).wait_recv()
    beam_ref[...] = jnp.sum(held[...], axis=1) * (1.0 / stations)
    for copy in sent:
        copy.wait_send()


def reduce_beam(part, ng, nr, nc, stations):
    def kernel(*refs):
        reduce_kernel(ng, nr, nc, stations, *refs)

    return pl.pallas_call(
        kernel,
        out_shape=jax.ShapeDtypeStruct((ng,) + part.shape[1:], jnp.float32),
        in_specs=[pl.BlockSpec(memory_space=pltpu.VMEM)],
        out_specs=pl.BlockSpec(memory_space=pltpu.VMEM),
        scratch_shapes=[
            pltpu.VMEM((ng, nr * nc) + part.shape[1:], jnp.float32),
            pltpu.SemaphoreType.DMA((ng, nr * nc)),
            pltpu.SemaphoreType.DMA((ng, nr * nc)),
        ],
        compiler_params=pltpu.CompilerParams(collective_id=1, has_side_effects=True),
        name="reduce_beam",
    )(part)


def body(nw, nr, nc, spectra, bins, travel):
    w, r, c = lax.axis_index("win"), lax.axis_index("srow"), lax.axis_index("scol")
    group, core = w // 2, w % 2
    nf, _, wl, n = spectra.shape
    half_f = nf // 2
    ph = travel.shape[1] // 2
    x = phase_normalized(spectra).reshape(half_f, 2, 2, wl, n).swapaxes(0, 1)
    t = (travel % NFFT).astype(jnp.int16).reshape(n, 2, ph).swapaxes(0, 1)
    xg, tcol, trow = exchange(x, t, nw, nr, nc)
    cols = xg[:, :nr].transpose(2, 1, 3, 0, 4, 5)
    xcr = cols.reshape(half_f, nr, 2 * nw * wl, n)
    xci = jnp.stack([-cols[:, :, 1], cols[:, :, 0]], axis=2).reshape(half_f, nr, 2 * nw * wl, n)
    xrow = xg[:, nr:].transpose(2, 1, 5, 3, 0, 4).reshape(half_f, nc * n, 2 * nw * wl)
    info = jnp.concatenate([
        jnp.stack([r, group]).astype(jnp.int32),
        jnp.stack([bins[(group + i) % half_f * 2 + core] for i in range(half_f)]),
        c[None].astype(jnp.int32),
    ])
    coherent, part = beam_call(info, xrow, xcr, xci, tcol, trow, nw * wl)
    part = part.sum(axis=2).reshape(half_f, 2, 2, ph).swapaxes(1, 2).reshape(half_f, 4 * ph // 128, 128)
    beam = reduce_beam(part, nw // 2, nr, nc, nr * nc * n).reshape(1, 2 * nw * ph)
    return coherent.transpose(0, 2, 1, 3)[None], beam


def solution(mesh):
    sizes = [mesh.shape[a] for a in ("win", "srow", "scol")]
    placed = (P(None, None, "win", ("srow", "scol")), P(), P(("srow", "scol"), "win"))
    return jax.shard_map(
        functools.partial(body, *sizes),
        mesh=mesh,
        in_specs=placed,
        out_specs=(P("win", None, "srow", None, "scol"), P("win", None)),
        check_vma=False,
    )
```
